512 devices in a mesh: corpus: 32 (over y, x, core), conv: 16 (over z).
Axes of the slice: x: 4, y: 4, z: 16, core: 2. Of those that a mesh axis runs over, the one named last changes fastest.
Arguments:
- queries: bfloat16 [65536, 2048], P(('corpus', 'conv')), may hold values from -128 to 128
- cotangent: bfloat16 [65536, 2048], P(('corpus', 'conv')), may hold values from -6 to 6
- corpus_of: int32 [65536, 1], P(('corpus', 'conv')), may hold values from 0 to 31, as said below
- cartridge: bfloat16 [32, 2048, 1024], P('corpus', 'conv'), may hold values from -6 to 6
Outputs:
- attended: bfloat16 [65536, 2048], P(('corpus', 'conv'))
- cartridge_grad: float32 [32, 2048, 1024], P('corpus', 'conv')
The draws below stay inside these ranges and needn't reach their ends.
Inputs may be any that keep to these rules, and one draw needn't show every extreme that they name: `corpus_of`: every block of 128 rows holds the same labels: token t belongs to conversation t % 128, and each conversation to one corpus. Every corpus has 1 to 5 conversations, and some corpus exactly 5.
All inputs are finite; a program needn't handle non-finite values.
Results may differ from the reference program's by a relative error of at most 0.03.
Values may be sent and summed in bfloat16 or wider, within the bound.
No kernel may reach another device: no remote copies, remote signals or barrier semaphores. Data moves between devices by JAX's collectives and lax.ppermute only.
A program may use at most 128 MiB of HBM per device.

```python
import jax
import jax.numpy as jnp
from jax import lax

HEADS = 16
KV_HEADS = 4
HEAD_DIM = 128
ROWS = 2048
TOK_DEV = 128
CORPORA = 32
CAP = 5
TOKENS = 65536
N_CORPUS = 32
N_CONV = 16


def draw_queries(key, part):
    key = jax.random.fold_in(key, 1)
    values = jnp.clip(jax.random.normal(key, (TOKENS, HEADS * HEAD_DIM), jnp.float32), -6.0, 6.0)
    return values.astype(jnp.bfloat16)


def draw_corpus_of(key, part):
    key = jax.random.fold_in(key, 3)
    first, second = jax.random.split(key)
    order = jax.random.permutation(first, CORPORA).astype(jnp.int32)
    extra = TOK_DEV - CORPORA
    ranking = jnp.arange(CORPORA, dtype=jnp.int32)
    counts = (1 + jnp.clip(extra - (CAP - 1) * ranking, 0, CAP - 1)).astype(jnp.int32)
    labels = jnp.repeat(order, counts, total_repeat_length=TOK_DEV)
    labels = jax.random.permutation(second, labels)
    return jnp.tile(labels, TOKENS // TOK_DEV)[:, None].astype(jnp.int32)


def draw_cartridge(key, part):
    kv_width = KV_HEADS * HEAD_DIM
    key = jax.random.fold_in(key, 2)
    values = jnp.clip(jax.random.normal(key, (CORPORA, ROWS, 2 * kv_width), jnp.float32), -6.0, 6.0)
    return values.astype(jnp.bfloat16)


def level_of(stream_key, shape, shards, smallest, top_value):
    factor_of = 1.0
    for position, shards_of in shards:
        heights = jax.random.uniform(jax.random.fold_in(jax.random.fold_in(stream_key, 6), position), (shards_of,), jnp.float32, smallest / len(shards), top_value / len(shards))
        factor_of = factor_of * jnp.repeat(jnp.exp(heights), shape[position] // shards_of).reshape((-1,) + (1,) * (len(shape) - 1 - position))
    return factor_of


def noise(own_key, dims, spread, bound, pieces=(), kind=jnp.bfloat16):
    loudness = level_of(own_key, dims, pieces, -0.22, 0.18) if pieces else 1.0
    result = jax.random.normal(own_key, dims, jnp.float32) * spread * loudness
    return jnp.minimum(jnp.maximum(result, -bound), bound).astype(kind)


def setup_inputs(seed: int = 0) -> dict:
    seeds = jax.random.split(jax.random.key(seed), 5)
    queries = draw_queries(jax.random.fold_in(seeds[4], 71), 0)
    cotangent = noise(seeds[1], (TOKENS, HEADS * HEAD_DIM), 1.0, 6.0, ((0, 512),))
    corpus_of = draw_corpus_of(jax.random.fold_in(seeds[4], 71), 0)
    cartridge = draw_cartridge(jax.random.fold_in(seeds[4], 71), 0)
    return dict(queries=queries, cotangent=cotangent, corpus_of=corpus_of, cartridge=cartridge)


def rounded(values):
    return lax.optimization_barrier(values.astype(jnp.bfloat16)).astype(jnp.float32)


def attend(query_rows, grad_rows, key_rows, value_rows):
    slot_count = query_rows.shape[0]
    per_group = HEADS // KV_HEADS
    score_scale = HEAD_DIM ** -0.5
    query_heads = query_rows.reshape(slot_count, KV_HEADS, per_group, HEAD_DIM).astype(jnp.float32)
    grad_heads = grad_rows.reshape(slot_count, KV_HEADS, per_group, HEAD_DIM).astype(jnp.float32)
    outputs = []
    key_grads = []
    value_grads = []
    for head in range(KV_HEADS):
        key_head = key_rows[:, head * HEAD_DIM:(head + 1) * HEAD_DIM].astype(jnp.float32)
        value_head = value_rows[:, head * HEAD_DIM:(head + 1) * HEAD_DIM].astype(jnp.float32)
        scores = jnp.einsum("sgd,rd->sgr", query_heads[:, head], key_head) * score_scale
        row_max = jnp.max(scores, axis=2, keepdims=True)
        weights = jnp.exp(scores - row_max)
        probs = rounded(weights / jnp.sum(weights, axis=2, keepdims=True))
        head_out = jnp.einsum("sgr,rd->sgd", probs, value_head)
        row_delta = jnp.sum(grad_heads[:, head] * head_out, axis=2, keepdims=True)
        value_grads.append(jnp.einsum("sgr,sgd->rd", probs, grad_heads[:, head]))
        prob_grad = jnp.einsum("sgd,rd->sgr", grad_heads[:, head], value_head)
        score_grad = rounded(probs * (prob_grad - row_delta))
        key_grads.append(jnp.einsum("sgr,sgd->rd", score_grad, query_heads[:, head]) * score_scale)
        outputs.append(head_out)
    head_outs = jnp.stack(outputs, axis=1).reshape(slot_count, HEADS * HEAD_DIM)
    return head_outs, jnp.concatenate(key_grads + value_grads, axis=1)


def reference(queries, cotangent, corpus_of, cartridge):
    tokens = queries.shape[0]
    groups = CORPORA * N_CONV
    window = N_CORPUS * CAP
    kv_width = cartridge.shape[2] // 2
    target = corpus_of[:, 0].astype(jnp.int32)
    column_ids = ((jnp.arange(tokens, dtype=jnp.int32) // TOK_DEV) % N_CONV).astype(jnp.int32)
    group_label = (target * N_CONV + column_ids).astype(jnp.int32)
    ordering = jnp.argsort(group_label, stable=True).astype(jnp.int32)
    counts = jax.ops.segment_sum(jnp.ones((tokens,), jnp.int32), group_label, num_segments=groups).astype(jnp.int32)
    starts = (jnp.cumsum(counts) - counts).astype(jnp.int32)
    feature = queries.shape[1]
    padded_queries = jnp.concatenate([queries[ordering], jnp.zeros((window, feature), queries.dtype)], axis=0)
    padded_grads = jnp.concatenate([cotangent[ordering], jnp.zeros((window, feature), cotangent.dtype)], axis=0)

    def corpus_step(corpus):
        key_rows = cartridge[corpus, :, :kv_width]
        value_rows = cartridge[corpus, :, kv_width:]

        def column_step(column):
            group_id = (corpus * N_CONV + column).astype(jnp.int32)
            group_start = starts[group_id]
            group_size = counts[group_id]
            live_rows = (jnp.arange(window, dtype=jnp.int32) < group_size)[:, None]
            query_rows = jnp.where(live_rows, lax.dynamic_slice_in_dim(padded_queries, group_start, window, 0), 0)
            grad_rows = jnp.where(live_rows, lax.dynamic_slice_in_dim(padded_grads, group_start, window, 0), 0)
            head_outs, grad_term = attend(query_rows, grad_rows, key_rows, value_rows)
            return head_outs.astype(jnp.bfloat16), grad_term.astype(jnp.bfloat16)

        group_outs, group_terms = lax.map(column_step, jnp.arange(N_CONV, dtype=jnp.int32))
        return group_outs, jnp.sum(group_terms.astype(jnp.float32), axis=0)

    all_outs, cartridge_grad = lax.map(corpus_step, jnp.arange(CORPORA, dtype=jnp.int32))
    flattened = all_outs.reshape(groups * window, feature)
    sorted_label = group_label[ordering]
    rank_in_group = jnp.arange(tokens, dtype=jnp.int32) - starts[sorted_label]
    picked = flattened[(sorted_label * window + rank_in_group).astype(jnp.int32)]
    attended = jnp.zeros_like(picked).at[ordering].set(picked)
    return attended, cartridge_grad
```

```python
import functools

import jax
import jax.numpy as jnp
from jax import lax
from jax.experimental import pallas as pl
from jax.experimental.pallas import tpu as pltpu
from jax.sharding import PartitionSpec as P

HEAD_DIM = 128
KV_HEADS = 4
GROUP = 4
CAP = 5
OWNERS = 32
RING = 16
ROWS = 2048
SHARD = ROWS // RING
TOK = 128
SLAB = OWNERS * 8
QUERIES = OWNERS * CAP * GROUP
BLOCK = 512
SCALE = HEAD_DIM ** -0.5
EXP2_SCALE = SCALE * 1.4426950408889634
RECV_STEP = 5
DONE_STEP = 7
VMEM_LIMIT = 56 * 1024 * 1024

f32 = jnp.float32
bf16 = jnp.bfloat16


def dot(a, b):
    return jnp.dot(a, b, preferred_element_type=f32)


def iota(shape, dim):
    return lax.broadcasted_iota(jnp.int32, shape, dim)


def one_hot(mask):
    return jnp.where(mask, 1.0, 0.0).astype(bf16)


def bases(owner, rank):
    out = []
    for first in (0, 2):
        here = (rank >= first) & (rank < first + 2)
        out.append(jnp.where(here, owner * 8 + (rank - first) * 4, -64))
    out.append(jnp.where(rank == 4, owner * 8, -64))
    return out


def pack_kernel(row_ref, col_ref, q_ref, c_ref, out_ref):
    row = row_ref[...]
    same = jnp.broadcast_to(col_ref[...], (TOK, TOK)) == jnp.broadcast_to(row, (TOK, TOK))
    before = iota((TOK, TOK), 0) < iota((TOK, TOK), 1)
    rank = jnp.sum(jnp.where(same & before, 1, 0), axis=0, keepdims=True)
    base = bases(row, rank)
    slab_row = iota((SLAB, TOK), 0)

    def place(first, count):
        wide = jnp.broadcast_to(first, (SLAB, TOK))
        return jnp.concatenate([one_hot(slab_row == wide + j) for j in range(count)], axis=1)

    def head(ref, h):
        return ref[:, h * HEAD_DIM:(h + 1) * HEAD_DIM]

    full = jnp.concatenate(
        [jnp.concatenate([head(r, 4 * k + j) for r in (q_ref, c_ref) for k in range(4)], axis=1) for j in range(4)],
        axis=0,
    )
    for g in range(2):
        slab = dot(place(base[g], 4), full).astype(bf16)
        out_ref[:, g * 512:(g + 1) * 512] = slab[:, :512]
        out_ref[:, 1280 + g * 512:1280 + (g + 1) * 512] = slab[:, 512:]
    last = jnp.concatenate(
        [
            jnp.concatenate([head(r, 4 * (2 * kp + kk) + j) for r in (q_ref, c_ref) for kp in range(2)], axis=1)
            for kk in range(2)
            for j in range(4)
        ],
        axis=0,
    )
    slab = dot(place(base[2], 8), last).astype(bf16)
    out_ref[:, 1024:1280] = slab[:, :256]
    out_ref[:, 2304:2560] = slab[:, 256:]


def unpack_kernel(row_ref, col_ref, in_ref, out_ref):
    col = col_ref[...]
    same = jnp.broadcast_to(col, (TOK, TOK)) == jnp.broadcast_to(row_ref[...], (TOK, TOK))
    before = iota((TOK, TOK), 1) < iota((TOK, TOK), 0)
    rank = jnp.sum(jnp.where(same & before, 1, 0), axis=1, keepdims=True)
    base = bases(col, rank)
    slab_col = iota((TOK, SLAB), 1)

    def pick(first, count):
        wide = jnp.broadcast_to(first, (TOK, SLAB))
        return jnp.concatenate([one_hot(slab_col == wide + j) for j in range(count)], axis=0)

    total = None
    for g in range(2):
        slab = jnp.concatenate([in_ref[:, g * 256:(g + 1) * 256], in_ref[:, 640 + g * 256:640 + (g + 1) * 256]], axis=1)
        part = dot(pick(base[g], 4), slab)
        total = part if total is None else total + part
    last = dot(pick(base[2], 8), jnp.concatenate([in_ref[:, 512:640], in_ref[:, 1152:1280]], axis=1))
    for k in range(4):
        for j in range(4):
            h = 4 * k + j
            first = ((k % 2) * 4 + j) * TOK
            value = total[j * TOK:(j + 1) * TOK, k * 128:(k + 1) * 128]
            value = value + last[first:first + TOK, (k // 2) * 128:(k // 2 + 1) * 128]
            out_ref[:, h * HEAD_DIM:(h + 1) * HEAD_DIM] = value.astype(bf16)


def attend(group, rolled, z, recv_ref, kv_ref, out_ref, out_lane, grad_ref, q_s, c_s, qt_s, ct_s, s_s, w_s, acc_s):
    half_row = iota((SLAB // 2, SLAB), 0)
    half_col = iota((SLAB // 2, SLAB), 1)
    back_row = iota((SLAB, SLAB // 2), 0)
    back_col = iota((SLAB, SLAB // 2), 1)
    tail = None
    for kk in range(2):
        k = 2 * group + kk
        take = one_hot(half_col == (half_row // 4) * 8 + kk * 4 + half_row % 4)
        give = one_hot(back_row == (back_col // 4) * 8 + kk * 4 + back_col % 4)
        for ref, first in ((q_s, 0), (c_s, 1280)):
            ref[0:256, :] = recv_ref[:, first + k * 128:first + (k + 1) * 128]
            ref[256:512, :] = recv_ref[:, first + 512 + k * 128:first + 512 + (k + 1) * 128]
            ref[512:640, :] = dot(take, recv_ref[:, first + 1024 + group * 128:first + 1024 + (group + 1) * 128]).astype(bf16)
        qt_s[...] = q_s[...].astype(f32).T.astype(bf16)
        key = slice(kk * 128, (kk + 1) * 128)
        val = slice(256 + kk * 128, 256 + (kk + 1) * 128)

        def score_step(i, top):
            rows = pl.ds(pl.multiple_of(i * BLOCK, BLOCK), BLOCK)
            s = dot(kv_ref[rows, key], qt_s[...])
            s_s[rows, :] = s
            return jnp.maximum(top, jnp.max(s, axis=0, keepdims=True))

        top = lax.fori_loop(0, ROWS // BLOCK, score_step, jnp.full((1, QUERIES), -jnp.inf, f32))
        top = top * EXP2_SCALE
        acc_s[...] = jnp.zeros_like(acc_s)

        def weight_step(i, total):
            rows = pl.ds(pl.multiple_of(i * BLOCK, BLOCK), BLOCK)
            w = jnp.exp2(s_s[rows, :] * EXP2_SCALE - top)
            wb = w.astype(bf16)
            w_s[rows, :] = wb
            vt = kv_ref[rows, val].astype(f32).T.astype(bf16)
            acc_s[...] += dot(vt, wb)
            return total + jnp.sum(w, axis=0, keepdims=True)

        total = lax.fori_loop(0, ROWS // BLOCK, weight_step, jnp.zeros((1, QUERIES), f32))
        inverse = 1.0 / total
        out_t = acc_s[...] * inverse
        ct = (c_s[...].astype(f32).T * inverse).astype(bf16)
        ct_s[...] = ct
        delta = jnp.sum(ct.astype(f32) * out_t, axis=0, keepdims=True)
        c_s[...] = ct.astype(f32).T.astype(bf16)
        out = out_t.T.astype(bf16)
        out_ref[:, out_lane + kk * 128:out_lane + (kk + 1) * 128] = out[0:256, :]
        out_ref[:, out_lane + 256 + kk * 128:out_lane + 256 + (kk + 1) * 128] = out[256:512, :]
        part = dot(give, out[512:640, :])
        tail = part if tail is None else tail + part

        def grad_step(i, carry):
            rows = pl.ds(pl.multiple_of(i * BLOCK, BLOCK), BLOCK)
            wb = w_s[rows, :]
            prob_grad = dot(kv_ref[rows, val], ct_s[...])
            ds = (wb.astype(f32) * (prob_grad - delta)).astype(bf16)
            value_grad = dot(wb, c_s[...]).astype(bf16)
            key_grad = (dot(ds, q_s[...]) * SCALE).astype(bf16)
            for sub in range(BLOCK // SHARD):
                at = i * (BLOCK // SHARD) + sub
                if rolled:
                    at = lax.rem(at - z + RING, RING)
                to = pl.ds(pl.multiple_of(at * SHARD, SHARD), SHARD)
                grad_ref[to, key] = key_grad[sub * SHARD:(sub + 1) * SHARD, :]
                grad_ref[to, val] = value_grad[sub * SHARD:(sub + 1) * SHARD, :]
            return carry

        lax.fori_loop(0, ROWS // BLOCK, grad_step, 0)
    out_ref[:, out_lane + 512:out_lane + 640] = tail.astype(bf16)


def first_kernel(offsets, z_ref, recv_ref, *refs):
    blocks = refs[:RING]
    out_ref, grad_ref, kv_s = refs[RING:RING + 3]
    z = z_ref[0]
    for offset, block in zip(offsets, blocks):
        at = lax.rem(z + (offset + RING), RING)
        kv_s[pl.ds(pl.multiple_of(at * SHARD, SHARD), SHARD), :] = block[...]
    attend(0, False, z, recv_ref, kv_s, out_ref, 0, grad_ref, *refs[RING + 3:])


def second_kernel(z_ref, recv_ref, kv_ref, early_ref, out_ref, grad_ref, *scratch):
    out_ref[:, 0:640] = early_ref[...]
    attend(1, True, z_ref[0], recv_ref, kv_ref, out_ref, 640, grad_ref, *scratch)


def vmem(count):
    return [pl.BlockSpec(memory_space=pltpu.VMEM)] * count


SMEM = pl.BlockSpec(memory_space=pltpu.SMEM)
WORK = [
    pltpu.VMEM((QUERIES, HEAD_DIM), bf16),
    pltpu.VMEM((QUERIES, HEAD_DIM), bf16),
    pltpu.VMEM((HEAD_DIM, QUERIES), bf16),
    pltpu.VMEM((HEAD_DIM, QUERIES), bf16),
    pltpu.VMEM((ROWS, QUERIES), f32),
    pltpu.VMEM((ROWS, QUERIES), bf16),
    pltpu.VMEM((HEAD_DIM, QUERIES), f32),
]
PARAMS = pltpu.CompilerParams(vmem_limit_bytes=VMEM_LIMIT)
ATTEND_COST = pl.CostEstimate(
    flops=2 * 5 * 2 * QUERIES * ROWS * HEAD_DIM * 2, bytes_accessed=6 * 1024 * 1024, transcendentals=2 * QUERIES * ROWS
)
SMALL_COST = pl.CostEstimate(flops=2 * 1024 * 1024 * 1024, bytes_accessed=3 * 1024 * 1024, transcendentals=0)


def local(queries, cotangent, corpus_of, cartridge):
    forward = [(i, (i + 1) % RING) for i in range(RING)]
    backward = [(i, (i - 1) % RING) for i in range(RING)]
    z = lax.axis_index("conv").astype(jnp.int32).reshape(1)
    shard = cartridge[0]
    shard_a = jnp.concatenate([shard[:, 0:256], shard[:, 512:768]], axis=1)
    shard_b = jnp.concatenate([shard[:, 256:512], shard[:, 768:1024]], axis=1)
    gathered_b = lax.all_gather(shard_b, "conv", axis=0, tiled=True)

    col = corpus_of.astype(jnp.int32)
    row = col.reshape(1, TOK)
    packed = pl.pallas_call(
        pack_kernel,
        out_shape=jax.ShapeDtypeStruct((SLAB, 2560), bf16),
        in_specs=vmem(4),
        out_specs=vmem(1)[0],
        compiler_params=PARAMS,
        cost_estimate=SMALL_COST,
        name="pack",
    )(row, col, queries, cotangent)
    recv = lax.all_to_all(packed, "corpus", split_axis=0, concat_axis=0, tiled=True)

    blocks = [shard_a]
    offsets = [0]
    ahead = behind = shard_a
    for step in range(1, RING // 2 + 1):
        if step == RECV_STEP:
            ahead, behind, recv = lax.optimization_barrier((ahead, behind, recv))
        ahead = lax.ppermute(ahead, "conv", forward)
        blocks.append(ahead)
        offsets.append(-step)
        if step < RING // 2:
            behind = lax.ppermute(behind, "conv", backward)
            blocks.append(behind)
            offsets.append(step)

    out_a, grad_a = pl.pallas_call(
        functools.partial(first_kernel, tuple(offsets)),
        out_shape=(jax.ShapeDtypeStruct((SLAB, 640), bf16), jax.ShapeDtypeStruct((ROWS, 512), bf16)),
        in_specs=[SMEM] + vmem(1 + RING),
        out_specs=tuple(vmem(2)),
        scratch_shapes=[pltpu.VMEM((ROWS, 512), bf16)] + WORK,
        compiler_params=PARAMS,
        cost_estimate=ATTEND_COST,
        name="attend_a",
    )(z, recv, *blocks)
    done_a = lax.psum_scatter(grad_a, "conv", scatter_dimension=0, tiled=True)

    out, grad_b = pl.pallas_call(
        second_kernel,
        out_shape=(jax.ShapeDtypeStruct((SLAB, 1280), bf16), jax.ShapeDtypeStruct((ROWS, 512), bf16)),
        in_specs=[SMEM] + vmem(3),
        out_specs=tuple(vmem(2)),
        scratch_shapes=WORK,
        compiler_params=PARAMS,
        cost_estimate=ATTEND_COST,
        name="attend_b",
    )(z, recv, gathered_b, out_a)

    def piece(index):
        return grad_b[index * SHARD:(index + 1) * SHARD, :].astype(f32)

    up = piece(8).astype(bf16)
    down = piece(9).astype(bf16)
    for step in range(1, RING // 2 + 1):
        if step == DONE_STEP:
            up, down, done_a = lax.optimization_barrier((up, down, done_a))
        up = lax.ppermute(up, "conv", forward)
        if step < RING // 2:
            up = (up.astype(f32) + piece(8 - step)).astype(bf16)
            down = lax.ppermute(down, "conv", backward)
            if step < RING // 2 - 1:
                down = (down.astype(f32) + piece(9 + step)).astype(bf16)
    done_b = piece(0) + up.astype(f32) + down.astype(f32)

    replies = lax.all_to_all(out, "corpus", split_axis=0, concat_axis=0, tiled=True)
    attended = pl.pallas_call(
        unpack_kernel,
        out_shape=jax.ShapeDtypeStruct((TOK, 2048), bf16),
        in_specs=vmem(3),
        out_specs=vmem(1)[0],
        compiler_params=PARAMS,
        cost_estimate=SMALL_COST,
        name="unpack",
    )(row, col, replies)
    done_a = done_a.astype(f32)
    grad = jnp.concatenate([done_a[:, 0:256], done_b[:, 0:256], done_a[:, 256:512], done_b[:, 256:512]], axis=1)
    return attended, grad[None]


def solution(mesh):
    return jax.shard_map(
        local,
        mesh=mesh,
        in_specs=(
            P(("corpus", "conv"), None),
            P(("corpus", "conv"), None),
            P(("corpus", "conv"), None),
            P("corpus", "conv", None),
        ),
        out_specs=(P(("corpus", "conv"), None), P("corpus", "conv", None)),
        check_vma=False,
    )
```

```python
import jax
import jax.numpy as jnp
from jax import lax
from jax.experimental import pallas as pl
from jax.experimental.pallas import tpu as pltpu
from jax.sharding import Mesh, PartitionSpec as P

HEAD_DIM = 128
GROUP = 4
CAP = 5
OWNERS = 32
PAIR = 2
ROWS = 2048
SHARD = 128
TOK = 128
SLAB = OWNERS * 8
RECV = PAIR * SLAB
QUERIES = PAIR * OWNERS * CAP * GROUP
BLOCK = 256
SCALE = HEAD_DIM ** -0.5
EXP2_SCALE = SCALE * 1.4426950408889634
VMEM_LIMIT = 56 * 1024 * 1024

f32 = jnp.float32
bf16 = jnp.bfloat16


def dot(a, b):
    return jnp.dot(a, b, preferred_element_type=f32)


def iota(shape, dim):
    return lax.broadcasted_iota(jnp.int32, shape, dim)


def one_hot(mask):
    return jnp.where(mask, 1.0, 0.0).astype(bf16)


def bases(owner, rank):
    out = []
    for first in (0, 2):
        here = (rank >= first) & (rank < first + 2)
        out.append(jnp.where(here, owner * 8 + (rank - first) * 4, -64))
    out.append(jnp.where(rank == 4, owner * 8, -64))
    return out


def pack_kernel(row_ref, col_ref, q_ref, c_ref, out_ref):
    row = row_ref[...]
    same = jnp.broadcast_to(col_ref[...], (TOK, TOK)) == jnp.broadcast_to(row, (TOK, TOK))
    before = iota((TOK, TOK), 0) < iota((TOK, TOK), 1)
    rank = jnp.sum(jnp.where(same & before, 1, 0), axis=0, keepdims=True)
    base = bases(row, rank)
    slab_row = iota((SLAB, TOK), 0)

    def place(first, count):
        wide = jnp.broadcast_to(first, (SLAB, TOK))
        return jnp.concatenate([one_hot(slab_row == wide + j) for j in range(count)], axis=1)

    def head(ref, h):
        return ref[:, h * HEAD_DIM:(h + 1) * HEAD_DIM]

    full = jnp.concatenate(
        [jnp.concatenate([head(r, 4 * k + j) for r in (q_ref, c_ref) for k in range(4)], axis=1) for j in range(4)],
        axis=0,
    )
    for g in range(2):
        slab = dot(place(base[g], 4), full).astype(bf16)
        for p in range(2):
            rows = slice(p * SLAB, (p + 1) * SLAB)
            out_ref[rows, g * 256:(g + 1) * 256] = slab[:, p * 256:(p + 1) * 256]
            out_ref[rows, 640 + g * 256:640 + (g + 1) * 256] = slab[:, 512 + p * 256:512 + (p + 1) * 256]
    last = jnp.concatenate(
        [
            jnp.concatenate([head(r, 4 * (2 * p + kk) + j) for r in (q_ref, c_ref) for p in range(2)], axis=1)
            for kk in range(2)
            for j in range(4)
        ],
        axis=0,
    )
    slab = dot(place(base[2], 8), last).astype(bf16)
    for p in range(2):
        rows = slice(p * SLAB, (p + 1) * SLAB)
        out_ref[rows, 512:640] = slab[:, p * 128:(p + 1) * 128]
        out_ref[rows, 1152:1280] = slab[:, 256 + p * 128:256 + (p + 1) * 128]


def unpack_kernel(row_ref, col_ref, in_ref, out_ref):
    col = col_ref[...]
    same = jnp.broadcast_to(col, (TOK, TOK)) == jnp.broadcast_to(row_ref[...], (TOK, TOK))
    before = iota((TOK, TOK), 1) < iota((TOK, TOK), 0)
    rank = jnp.sum(jnp.where(same & before, 1, 0), axis=1, keepdims=True)
    base = bases(col, rank)
    slab_col = iota((TOK, SLAB), 1)

    def pick(first, count):
        wide = jnp.broadcast_to(first, (TOK, SLAB))
        return jnp.concatenate([one_hot(slab_col == wide + j) for j in range(count)], axis=0)

    total = None
    for g in range(2):
        slab = jnp.concatenate([in_ref[0:SLAB, g * 256:(g + 1) * 256], in_ref[SLAB:RECV, g * 256:(g + 1) * 256]], axis=1)
        part = dot(pick(base[g], 4), slab)
        total = part if total is None else total + part
    last = dot(pick(base[2], 8), jnp.concatenate([in_ref[0:SLAB, 512:640], in_ref[SLAB:RECV, 512:640]], axis=1))
    for k in range(4):
        for j in range(4):
            h = 4 * k + j
            first = ((k % 2) * 4 + j) * TOK
            value = total[j * TOK:(j + 1) * TOK, k * 128:(k + 1) * 128]
            value = value + last[first:first + TOK, (k // 2) * 128:(k // 2 + 1) * 128]
            out_ref[:, h * HEAD_DIM:(h + 1) * HEAD_DIM] = value.astype(bf16)


def attend_kernel(recv_ref, kv_ref, out_ref, grad_ref, q_s, c_s, qt_s, ct_s, s_s, w_s, acc_s):
    half_row = iota((RECV // 2, RECV), 0)
    half_col = iota((RECV // 2, RECV), 1)
    back_row = iota((RECV, RECV // 2), 0)
    back_col = iota((RECV, RECV // 2), 1)
    lanes = [(slice(kk * 128, (kk + 1) * 128), slice(256 + kk * 128, 256 + (kk + 1) * 128)) for kk in range(2)]

    def rows_of(i):
        return pl.ds(pl.multiple_of(i * BLOCK, BLOCK), BLOCK)

    def load(kk):
        take = one_hot(half_col == (half_row // 4) * 8 + kk * 4 + half_row % 4)
        for ref, first in ((q_s, 0), (c_s, 640)):
            ref[kk, 0:RECV, :] = recv_ref[:, first + kk * 128:first + (kk + 1) * 128]
            ref[kk, RECV:2 * RECV, :] = recv_ref[:, first + 256 + kk * 128:first + 256 + (kk + 1) * 128]
            ref[kk, 2 * RECV:QUERIES, :] = dot(take, recv_ref[:, first + 512:first + 640]).astype(bf16)
        qt_s[kk] = q_s[kk].astype(f32).T.astype(bf16)
        acc_s[kk] = jnp.zeros((HEAD_DIM, QUERIES), f32)

    def score(kk, i, top):
        s = dot(kv_ref[rows_of(i), lanes[kk][0]], qt_s[kk])
        s_s[kk, rows_of(i), :] = s
        return jnp.maximum(top, jnp.max(s, axis=0, keepdims=True))

    def weigh(kk, i, top, total):
        w = jnp.exp2(s_s[kk, rows_of(i), :] * EXP2_SCALE - top)
        wb = w.astype(bf16)
        w_s[kk, rows_of(i), :] = wb
        vt = kv_ref[rows_of(i), lanes[kk][1]].astype(f32).T.astype(bf16)
        acc_s[kk] += dot(vt, wb)
        return total + jnp.sum(w, axis=0, keepdims=True)

    def finish(kk, total):
        inverse = 1.0 / total
        out_t = acc_s[kk] * inverse
        ct = (c_s[kk].astype(f32).T * inverse).astype(bf16)
        ct_s[kk] = ct
        c_s[kk] = ct.astype(f32).T.astype(bf16)
        out = out_t.T.astype(bf16)
        out_ref[:, kk * 128:(kk + 1) * 128] = out[0:RECV, :]
        out_ref[:, 256 + kk * 128:256 + (kk + 1) * 128] = out[RECV:2 * RECV, :]
        give = one_hot(back_row == (back_col // 4) * 8 + kk * 4 + back_col % 4)
        return jnp.sum(ct.astype(f32) * out_t, axis=0, keepdims=True), dot(give, out[2 * RECV:QUERIES, :])

    def grads(kk, i, delta):
        key, val = lanes[kk]
        wb = w_s[kk, rows_of(i), :]
        prob_grad = dot(kv_ref[rows_of(i), val], ct_s[kk])
        ds = (wb.astype(f32) * (prob_grad - delta)).astype(bf16)
        grad_ref[rows_of(i), val] = dot(wb, c_s[kk]).astype(bf16)
        grad_ref[rows_of(i), key] = (dot(ds, q_s[kk]) * SCALE).astype(bf16)

    steps = ROWS // BLOCK
    lowest = jnp.full((1, QUERIES), -jnp.inf, f32)
    zero = jnp.zeros((1, QUERIES), f32)

    load(0)
    top0 = lax.fori_loop(0, steps, lambda i, top: score(0, i, top), lowest) * EXP2_SCALE
    load(1)

    def second(i, carry):
        top, total = carry
        return score(1, i, top), weigh(0, i, top0, total)

    top1, total0 = lax.fori_loop(0, steps, second, (lowest, zero))
    top1 = top1 * EXP2_SCALE
    delta0, tail0 = finish(0, total0)

    def third(i, total):
        grads(0, i, delta0)
        return weigh(1, i, top1, total)

    total1 = lax.fori_loop(0, steps, third, zero)
    delta1, tail1 = finish(1, total1)
    out_ref[:, 512:640] = (tail0 + tail1).astype(bf16)

    def fourth(i, carry):
        grads(1, i, delta1)
        return carry

    lax.fori_loop(0, steps, fourth, 0)


def split_kernel(side_ref, in_ref, keep_ref, send_ref):
    def copy(to_ref, half):
        to_ref[:, 0:256] = in_ref[:, half * 256:(half + 1) * 256]
        to_ref[:, 256:512] = in_ref[:, 512 + half * 256:512 + (half + 1) * 256]

    for side in range(2):

        @pl.when(side_ref[0] == side)
        def _():
            copy(keep_ref, side)
            copy(send_ref, 1 - side)


def join_kernel(side_ref, own_ref, other_ref, out_ref):
    def copy(ref, half):
        out_ref[:, half * 256:(half + 1) * 256] = ref[0:SHARD, 0:256].astype(f32)
        out_ref[:, 512 + half * 256:512 + (half + 1) * 256] = ref[0:SHARD, 256:512].astype(f32)

    for side in range(2):

        @pl.when(side_ref[0] == side)
        def _():
            copy(own_ref, side)
            copy(other_ref, 1 - side)


def vmem(count):
    return [pl.BlockSpec(memory_space=pltpu.VMEM)] * count


SMEM = pl.BlockSpec(memory_space=pltpu.SMEM)
WORK = [
    pltpu.VMEM((2, QUERIES, HEAD_DIM), bf16),
    pltpu.VMEM((2, QUERIES, HEAD_DIM), bf16),
    pltpu.VMEM((2, HEAD_DIM, QUERIES), bf16),
    pltpu.VMEM((2, HEAD_DIM, QUERIES), bf16),
    pltpu.VMEM((2, ROWS, QUERIES), f32),
    pltpu.VMEM((2, ROWS, QUERIES), bf16),
    pltpu.VMEM((2, HEAD_DIM, QUERIES), f32),
]
PARAMS = pltpu.CompilerParams(vmem_limit_bytes=VMEM_LIMIT)
ATTEND_COST = pl.CostEstimate(
    flops=2 * 5 * QUERIES * ROWS * HEAD_DIM * 2, bytes_accessed=6 * 1024 * 1024, transcendentals=2 * QUERIES * ROWS
)
SMALL_COST = pl.CostEstimate(flops=2 * 1024 * 1024 * 1024, bytes_accessed=3 * 1024 * 1024, transcendentals=0)


def local(queries, cotangent, corpus_of, cartridge):
    side = lax.axis_index("zl").astype(jnp.int32).reshape(1)
    swap = [(0, 1), (1, 0)]
    keep, send = pl.pallas_call(
        split_kernel,
        out_shape=(jax.ShapeDtypeStruct((SHARD, 512), bf16), jax.ShapeDtypeStruct((SHARD, 512), bf16)),
        in_specs=[SMEM] + vmem(1),
        out_specs=tuple(vmem(2)),
        compiler_params=PARAMS,
        name="split",
    )(side, cartridge[0])
    taken = lax.ppermute(send, "zl", swap)
    gathered = lax.all_gather(jnp.concatenate([keep, taken], axis=0), "zh", axis=0, tiled=True)

    col = corpus_of.astype(jnp.int32)
    row = col.reshape(1, TOK)
    packed = pl.pallas_call(
        pack_kernel,
        out_shape=jax.ShapeDtypeStruct((RECV, 1280), bf16),
        in_specs=vmem(4),
        out_specs=vmem(1)[0],
        compiler_params=PARAMS,
        cost_estimate=SMALL_COST,
        name="pack",
    )(row, col, queries, cotangent)
    packed, taken = lax.optimization_barrier((packed, taken))
    recv = lax.all_to_all(packed, ("zl", "corpus"), split_axis=0, concat_axis=0, tiled=True)

    out, grads = pl.pallas_call(
        attend_kernel,
        out_shape=(jax.ShapeDtypeStruct((RECV, 640), bf16), jax.ShapeDtypeStruct((ROWS, 512), bf16)),
        in_specs=vmem(2),
        out_specs=tuple(vmem(2)),
        scratch_shapes=WORK,
        compiler_params=PARAMS,
        cost_estimate=ATTEND_COST,
        name="attend",
    )(recv, gathered)

    summed = lax.psum_scatter(grads, "zh", scatter_dimension=0, tiled=True)
    other = lax.ppermute(summed[SHARD:], "zl", swap)
    grad = pl.pallas_call(
        join_kernel,
        out_shape=jax.ShapeDtypeStruct((SHARD, 1024), f32),
        in_specs=[SMEM] + vmem(2),
        out_specs=vmem(1)[0],
        compiler_params=PARAMS,
        name="join",
    )(side, summed, other)

    replies = lax.all_to_all(out, ("zl", "corpus"), split_axis=0, concat_axis=0, tiled=True)
    attended = pl.pallas_call(
        unpack_kernel,
        out_shape=jax.ShapeDtypeStruct((TOK, 2048), bf16),
        in_specs=vmem(3),
        out_specs=vmem(1)[0],
        compiler_params=PARAMS,
        cost_estimate=SMALL_COST,
        name="unpack",
    )(row, col, replies)
    return attended, grad[None]


def solution(mesh):
    corpus, conv = mesh.devices.shape
    pairs = Mesh(mesh.devices.reshape(corpus, conv // PAIR, PAIR), ("corpus", "zh", "zl"))
    tokens = P(("corpus", "zh", "zl"), None)
    rows = P("corpus", ("zh", "zl"), None)
    return jax.shard_map(
        local,
        mesh=pairs,
        in_specs=(tokens, tokens, tokens, rows),
        out_specs=(tokens, rows),
        check_vma=False,
    )
```

```python
import jax
import jax.numpy as jnp
from jax import lax
from jax.experimental import pallas as pl
from jax.experimental.pallas import tpu as pltpu
from jax.sharding import Mesh, PartitionSpec as P

HEAD_DIM = 128
GROUP = 4
CAP = 5
OWNERS = 32
PAIR = 2
ROWS = 2048
SHARD = 128
TOK = 128
SLAB = OWNERS * 8
RECV = PAIR * SLAB
QUERIES = PAIR * OWNERS * CAP * GROUP
BLOCK = PAIR * SHARD
STRIP = 16
PIECES = BLOCK // STRIP
WIDE = PIECES * 512
SCALE = HEAD_DIM ** -0.5
EXP2_SCALE = SCALE * 1.4426950408889634
VMEM_LIMIT = 56 * 1024 * 1024

f32 = jnp.float32
bf16 = jnp.bfloat16


def dot(a, b):
    return jnp.dot(a, b, preferred_element_type=f32)


def iota(shape, dim):
    return lax.broadcasted_iota(jnp.int32, shape, dim)


def one_hot(mask):
    return jnp.where(mask, 1.0, 0.0).astype(bf16)


def bases(owner, rank):
    out = []
    for first in (0, 2):
        here = (rank >= first) & (rank < first + 2)
        out.append(jnp.where(here, owner * 8 + (rank - first) * 4, -64))
    out.append(jnp.where(rank == 4, owner * 8, -64))
    return out


def pack_kernel(row_ref, col_ref, q_ref, c_ref, out_ref):
    row = row_ref[...]
    same = jnp.broadcast_to(col_ref[...], (TOK, TOK)) == jnp.broadcast_to(row, (TOK, TOK))
    before = iota((TOK, TOK), 0) < iota((TOK, TOK), 1)
    rank = jnp.sum(jnp.where(same & before, 1, 0), axis=0, keepdims=True)
    base = bases(row, rank)
    slab_row = iota((SLAB, TOK), 0)

    def place(first, count):
        wide = jnp.broadcast_to(first, (SLAB, TOK))
        return jnp.concatenate([one_hot(slab_row == wide + j) for j in range(count)], axis=1)

    def head(ref, h):
        return ref[:, h * HEAD_DIM:(h + 1) * HEAD_DIM]

    full = jnp.concatenate(
        [jnp.concatenate([head(r, 4 * k + j) for r in (q_ref, c_ref) for k in range(4)], axis=1) for j in range(4)],
        axis=0,
    )
    for g in range(2):
        slab = dot(place(base[g], 4), full).astype(bf16)
        for p in range(2):
            rows = slice(p * SLAB, (p + 1) * SLAB)
            out_ref[rows, g * 256:(g + 1) * 256] = slab[:, p * 256:(p + 1) * 256]
            out_ref[rows, 640 + g * 256:640 + (g + 1) * 256] = slab[:, 512 + p * 256:512 + (p + 1) * 256]
    last = jnp.concatenate(
        [
            jnp.concatenate([head(r, 4 * (2 * p + kk) + j) for r in (q_ref, c_ref) for p in range(2)], axis=1)
            for kk in range(2)
            for j in range(4)
        ],
        axis=0,
    )
    slab = dot(place(base[2], 8), last).astype(bf16)
    for p in range(2):
        rows = slice(p * SLAB, (p + 1) * SLAB)
        out_ref[rows, 512:640] = slab[:, p * 128:(p + 1) * 128]
        out_ref[rows, 1152:1280] = slab[:, 256 + p * 128:256 + (p + 1) * 128]


def unpack_kernel(row_ref, col_ref, in_ref, out_ref):
    col = col_ref[...]
    same = jnp.broadcast_to(col, (TOK, TOK)) == jnp.broadcast_to(row_ref[...], (TOK, TOK))
    before = iota((TOK, TOK), 1) < iota((TOK, TOK), 0)
    rank = jnp.sum(jnp.where(same & before, 1, 0), axis=1, keepdims=True)
    base = bases(col, rank)
    slab_col = iota((TOK, SLAB), 1)

    def pick(first, count):
        wide = jnp.broadcast_to(first, (TOK, SLAB))
        return jnp.concatenate([one_hot(slab_col == wide + j) for j in range(count)], axis=0)

    total = None
    for g in range(2):
        slab = jnp.concatenate([in_ref[0:SLAB, g * 256:(g + 1) * 256], in_ref[SLAB:RECV, g * 256:(g + 1) * 256]], axis=1)
        part = dot(pick(base[g], 4), slab)
        total = part if total is None else total + part
    last = dot(pick(base[2], 8), jnp.concatenate([in_ref[0:SLAB, 512:640], in_ref[SLAB:RECV, 512:640]], axis=1))
    for k in range(4):
        for j in range(4):
            h = 4 * k + j
            first = ((k % 2) * 4 + j) * TOK
            value = total[j * TOK:(j + 1) * TOK, k * 128:(k + 1) * 128]
            value = value + last[first:first + TOK, (k // 2) * 128:(k // 2 + 1) * 128]
            out_ref[:, h * HEAD_DIM:(h + 1) * HEAD_DIM] = value.astype(bf16)


def attend_kernel(recv_ref, wide_ref, out_ref, grad_ref, kv_ref, q_s, c_s, qt_s, ct_s, s_s, w_s, acc_s):
    half_row = iota((RECV // 2, RECV), 0)
    half_col = iota((RECV // 2, RECV), 1)
    back_row = iota((RECV, RECV // 2), 0)
    back_col = iota((RECV, RECV // 2), 1)
    lanes = [(slice(kk * 128, (kk + 1) * 128), slice(256 + kk * 128, 256 + (kk + 1) * 128)) for kk in range(2)]

    def rows_of(i):
        return pl.ds(pl.multiple_of(i * BLOCK, BLOCK), BLOCK)

    def load(kk):
        take = one_hot(half_col == (half_row // 4) * 8 + kk * 4 + half_row % 4)
        for ref, first in ((q_s, 0), (c_s, 640)):
            ref[kk, 0:RECV, :] = recv_ref[:, first + kk * 128:first + (kk + 1) * 128]
            ref[kk, RECV:2 * RECV, :] = recv_ref[:, first + 256 + kk * 128:first + 256 + (kk + 1) * 128]
            ref[kk, 2 * RECV:QUERIES, :] = dot(take, recv_ref[:, first + 512:first + 640]).astype(bf16)
        qt_s[kk] = q_s[kk].astype(f32).T.astype(bf16)
        acc_s[kk] = jnp.zeros((HEAD_DIM, QUERIES), f32)

    def score(kk, i, top):
        s = dot(kv_ref[rows_of(i), lanes[kk][0]], qt_s[kk])
        s_s[kk, rows_of(i), :] = s
        return jnp.maximum(top, jnp.max(s, axis=0, keepdims=True))

    def weigh(kk, i, top, total):
        w = jnp.exp2(s_s[kk, rows_of(i), :] * EXP2_SCALE - top)
        wb = w.astype(bf16)
        w_s[kk, rows_of(i), :] = wb
        vt = kv_ref[rows_of(i), lanes[kk][1]].astype(f32).T.astype(bf16)
        acc_s[kk] += dot(vt, wb)
        return total + jnp.sum(w, axis=0, keepdims=True)

    def finish(kk, total):
        inverse = 1.0 / total
        out_t = acc_s[kk] * inverse
        ct = (c_s[kk].astype(f32).T * inverse).astype(bf16)
        ct_s[kk] = ct
        c_s[kk] = ct.astype(f32).T.astype(bf16)
        out = out_t.T.astype(bf16)
        out_ref[:, kk * 128:(kk + 1) * 128] = out[0:RECV, :]
        out_ref[:, 256 + kk * 128:256 + (kk + 1) * 128] = out[RECV:2 * RECV, :]
        give = one_hot(back_row == (back_col // 4) * 8 + kk * 4 + back_col % 4)
        return jnp.sum(ct.astype(f32) * out_t, axis=0, keepdims=True), dot(give, out[2 * RECV:QUERIES, :])

    def grads(kk, i, delta):
        key, val = lanes[kk]
        wb = w_s[kk, rows_of(i), :]
        prob_grad = dot(kv_ref[rows_of(i), val], ct_s[kk])
        ds = (wb.astype(f32) * (prob_grad - delta)).astype(bf16)
        value_grad = dot(wb, c_s[kk]).astype(bf16)
        key_grad = (dot(ds, q_s[kk]) * SCALE).astype(bf16)
        strip = pl.ds(pl.multiple_of(i * STRIP, STRIP), STRIP)
        for piece in range(PIECES):
            first = piece * 512 + kk * 128
            here = slice(piece * STRIP, (piece + 1) * STRIP)
            grad_ref[strip, first:first + 128] = key_grad[here, :]
            grad_ref[strip, first + 256:first + 384] = value_grad[here, :]

    steps = ROWS // BLOCK
    lowest = jnp.full((1, QUERIES), -jnp.inf, f32)
    zero = jnp.zeros((1, QUERIES), f32)

    def unfold(i, carry):
        strip = pl.ds(pl.multiple_of(i * STRIP, STRIP), STRIP)
        for piece in range(PIECES):
            to = pl.ds(pl.multiple_of(i * BLOCK + piece * STRIP, STRIP), STRIP)
            kv_ref[to, :] = wide_ref[strip, piece * 512:(piece + 1) * 512]
        return carry

    lax.fori_loop(0, steps, unfold, 0)
    load(0)
    top0 = lax.fori_loop(0, steps, lambda i, top: score(0, i, top), lowest) * EXP2_SCALE
    load(1)

    def second(i, carry):
        top, total = carry
        return score(1, i, top), weigh(0, i, top0, total)

    top1, total0 = lax.fori_loop(0, steps, second, (lowest, zero))
    top1 = top1 * EXP2_SCALE
    delta0, tail0 = finish(0, total0)

    def third(i, total):
        grads(0, i, delta0)
        return weigh(1, i, top1, total)

    total1 = lax.fori_loop(0, steps, third, zero)
    delta1, tail1 = finish(1, total1)
    out_ref[:, 512:640] = (tail0 + tail1).astype(bf16)

    def fourth(i, carry):
        grads(1, i, delta1)
        return carry

    lax.fori_loop(0, steps, fourth, 0)


def split_kernel(side_ref, in_ref, keep_ref, send_ref):
    def copy(to_ref, half):
        for piece in range(PIECES // 2):
            rows = slice(piece * STRIP, (piece + 1) * STRIP)
            first = piece * 512
            to_ref[:, first:first + 256] = in_ref[rows, half * 256:(half + 1) * 256]
            to_ref[:, first + 256:first + 512] = in_ref[rows, 512 + half * 256:512 + (half + 1) * 256]

    for side in range(2):

        @pl.when(side_ref[0] == side)
        def _():
            copy(keep_ref, side)
            copy(send_ref, 1 - side)


def join_kernel(side_ref, own_ref, other_ref, out_ref):
    def copy(ref, half):
        for piece in range(PIECES // 2):
            rows = slice(piece * STRIP, (piece + 1) * STRIP)
            first = piece * 512
            out_ref[rows, half * 256:(half + 1) * 256] = ref[:, first:first + 256].astype(f32)
            out_ref[rows, 512 + half * 256:512 + (half + 1) * 256] = ref[:, first + 256:first + 512].astype(f32)

    for side in range(2):

        @pl.when(side_ref[0] == side)
        def _():
            copy(own_ref, side)
            copy(other_ref, 1 - side)


def vmem(count):
    return [pl.BlockSpec(memory_space=pltpu.VMEM)] * count


SMEM = pl.BlockSpec(memory_space=pltpu.SMEM)
WORK = [
    pltpu.VMEM((ROWS, 512), bf16),
    pltpu.VMEM((2, QUERIES, HEAD_DIM), bf16),
    pltpu.VMEM((2, QUERIES, HEAD_DIM), bf16),
    pltpu.VMEM((2, HEAD_DIM, QUERIES), bf16),
    pltpu.VMEM((2, HEAD_DIM, QUERIES), bf16),
    pltpu.VMEM((2, ROWS, QUERIES), f32),
    pltpu.VMEM((2, ROWS, QUERIES), bf16),
    pltpu.VMEM((2, HEAD_DIM, QUERIES), f32),
]
PARAMS = pltpu.CompilerParams(vmem_limit_bytes=VMEM_LIMIT)
ATTEND_COST = pl.CostEstimate(
    flops=2 * 5 * QUERIES * ROWS * HEAD_DIM * 2, bytes_accessed=6 * 1024 * 1024, transcendentals=2 * QUERIES * ROWS
)
SMALL_COST = pl.CostEstimate(flops=2 * 1024 * 1024 * 1024, bytes_accessed=3 * 1024 * 1024, transcendentals=0)


def local(queries, cotangent, corpus_of, cartridge):
    side = lax.axis_index("zl").astype(jnp.int32).reshape(1)
    swap = [(0, 1), (1, 0)]
    keep, send = pl.pallas_call(
        split_kernel,
        out_shape=(jax.ShapeDtypeStruct((STRIP, WIDE // 2), bf16), jax.ShapeDtypeStruct((STRIP, WIDE // 2), bf16)),
        in_specs=[SMEM] + vmem(1),
        out_specs=tuple(vmem(2)),
        compiler_params=PARAMS,
        name="split",
    )(side, cartridge[0])
    taken = lax.ppermute(send, "zl", swap)
    both = jnp.concatenate([keep, taken], axis=1)
    gathered = lax.all_gather(both, "zh", axis=0, tiled=True)

    col = corpus_of.astype(jnp.int32)
    row = col.reshape(1, TOK)
    packed = pl.pallas_call(
        pack_kernel,
        out_shape=jax.ShapeDtypeStruct((RECV, 1280), bf16),
        in_specs=vmem(4),
        out_specs=vmem(1)[0],
        compiler_params=PARAMS,
        cost_estimate=SMALL_COST,
        name="pack",
    )(row, col, queries, cotangent)
    packed, both = lax.optimization_barrier((packed, both))
    recv = lax.all_to_all(packed, ("zl", "corpus"), split_axis=0, concat_axis=0, tiled=True)

    out, grads = pl.pallas_call(
        attend_kernel,
        out_shape=(jax.ShapeDtypeStruct((RECV, 640), bf16), jax.ShapeDtypeStruct((ROWS // PIECES, WIDE), bf16)),
        in_specs=vmem(2),
        out_specs=tuple(vmem(2)),
        scratch_shapes=WORK,
        compiler_params=PARAMS,
        cost_estimate=ATTEND_COST,
        name="attend",
    )(recv, gathered)

    summed = lax.psum_scatter(grads, "zh", scatter_dimension=0, tiled=True)
    replies = lax.all_to_all(out, ("zl", "corpus"), split_axis=0, concat_axis=0, tiled=True)
    attended = pl.pallas_call(
        unpack_kernel,
        out_shape=jax.ShapeDtypeStruct((TOK, 2048), bf16),
        in_specs=vmem(3),
        out_specs=vmem(1)[0],
        compiler_params=PARAMS,
        cost_estimate=SMALL_COST,
        name="unpack",
    )(row, col, replies)
    summed, attended = lax.optimization_barrier((summed, attended))
    other = lax.ppermute(summed[:, WIDE // 2:], "zl", swap)
    grad = pl.pallas_call(
        join_kernel,
        out_shape=jax.ShapeDtypeStruct((SHARD, 1024), f32),
        in_specs=[SMEM] + vmem(2),
        out_specs=vmem(1)[0],
        compiler_params=PARAMS,
        name="join",
    )(side, summed, other)

    return attended, grad[None]


def solution(mesh):
    corpus, conv = mesh.devices.shape
    pairs = Mesh(mesh.devices.reshape(corpus, conv // PAIR, PAIR), ("corpus", "zh", "zl"))
    tokens = P(("corpus", "zh", "zl"), None)
    rows = P("corpus", ("zh", "zl"), None)
    return jax.shard_map(
        local,
        mesh=pairs,
        in_specs=(tokens, tokens, tokens, rows),
        out_specs=(tokens, rows),
        check_vma=False,
    )
```

```python
import jax
import jax.numpy as jnp
from jax import lax
from jax.experimental import pallas as pl
from jax.experimental.pallas import tpu as pltpu
from jax.sharding import Mesh, PartitionSpec as P

HEAD_DIM = 128
GROUP = 4
CAP = 5
OWNERS = 32
PAIR = 2
ROWS = 2048
SHARD = 128
TOK = 128
SLAB = OWNERS * 8
RECV = PAIR * SLAB
QUERIES = PAIR * OWNERS * CAP * GROUP
BLOCK = 256
UNROLL = 2
SCALE = HEAD_DIM ** -0.5
EXP2_SCALE = SCALE * 1.4426950408889634
VMEM_LIMIT = 56 * 1024 * 1024

f32 = jnp.float32
bf16 = jnp.bfloat16


def dot(a, b):
    return jnp.dot(a, b, preferred_element_type=f32)


def iota(shape, dim):
    return lax.broadcasted_iota(jnp.int32, shape, dim)


def one_hot(mask):
    return jnp.where(mask, 1.0, 0.0).astype(bf16)


def bases(owner, rank):
    out = []
    for first in (0, 2):
        here = (rank >= first) & (rank < first + 2)
        out.append(jnp.where(here, owner * 8 + (rank - first) * 4, -64))
    out.append(jnp.where(rank == 4, owner * 8, -64))
    return out


def pack_kernel(row_ref, col_ref, q_ref, c_ref, out_ref):
    row = row_ref[...]
    same = jnp.broadcast_to(col_ref[...], (TOK, TOK)) == jnp.broadcast_to(row, (TOK, TOK))
    before = iota((TOK, TOK), 0) < iota((TOK, TOK), 1)
    rank = jnp.sum(jnp.where(same & before, 1, 0), axis=0, keepdims=True)
    base = bases(row, rank)
    slab_row = iota((SLAB, TOK), 0)

    def place(first, count):
        wide = jnp.broadcast_to(first, (SLAB, TOK))
        return jnp.concatenate([one_hot(slab_row == wide + j) for j in range(count)], axis=1)

    def head(ref, h):
        return ref[:, h * HEAD_DIM:(h + 1) * HEAD_DIM]

    full = jnp.concatenate(
        [jnp.concatenate([head(r, 4 * k + j) for r in (q_ref, c_ref) for k in range(4)], axis=1) for j in range(4)],
        axis=0,
    )
    for g in range(2):
        slab = dot(place(base[g], 4), full).astype(bf16)
        for p in range(2):
            rows = slice(p * SLAB, (p + 1) * SLAB)
            out_ref[rows, g * 256:(g + 1) * 256] = slab[:, p * 256:(p + 1) * 256]
            out_ref[rows, 640 + g * 256:640 + (g + 1) * 256] = slab[:, 512 + p * 256:512 + (p + 1) * 256]
    last = jnp.concatenate(
        [
            jnp.concatenate([head(r, 4 * (2 * p + kk) + j) for r in (q_ref, c_ref) for p in range(2)], axis=1)
            for kk in range(2)
            for j in range(4)
        ],
        axis=0,
    )
    slab = dot(place(base[2], 8), last).astype(bf16)
    for p in range(2):
        rows = slice(p * SLAB, (p + 1) * SLAB)
        out_ref[rows, 512:640] = slab[:, p * 128:(p + 1) * 128]
        out_ref[rows, 1152:1280] = slab[:, 256 + p * 128:256 + (p + 1) * 128]


def unpack_kernel(row_ref, col_ref, in_ref, out_ref):
    col = col_ref[...]
    same = jnp.broadcast_to(col, (TOK, TOK)) == jnp.broadcast_to(row_ref[...], (TOK, TOK))
    before = iota((TOK, TOK), 1) < iota((TOK, TOK), 0)
    rank = jnp.sum(jnp.where(same & before, 1, 0), axis=1, keepdims=True)
    base = bases(col, rank)
    slab_col = iota((TOK, SLAB), 1)

    def pick(first, count):
        wide = jnp.broadcast_to(first, (TOK, SLAB))
        return jnp.concatenate([one_hot(slab_col == wide + j) for j in range(count)], axis=0)

    total = None
    for g in range(2):
        slab = jnp.concatenate([in_ref[0:SLAB, g * 256:(g + 1) * 256], in_ref[SLAB:RECV, g * 256:(g + 1) * 256]], axis=1)
        part = dot(pick(base[g], 4), slab)
        total = part if total is None else total + part
    last = dot(pick(base[2], 8), jnp.concatenate([in_ref[0:SLAB, 512:640], in_ref[SLAB:RECV, 512:640]], axis=1))
    for k in range(4):
        for j in range(4):
            h = 4 * k + j
            first = ((k % 2) * 4 + j) * TOK
            value = total[j * TOK:(j + 1) * TOK, k * 128:(k + 1) * 128]
            value = value + last[first:first + TOK, (k // 2) * 128:(k // 2 + 1) * 128]
            out_ref[:, h * HEAD_DIM:(h + 1) * HEAD_DIM] = value.astype(bf16)


def attend_kernel(side_ref, recv_ref, all_ref, out_ref, grad_ref, kv_ref, *refs):
    q_s, c_s, qt_s, ct_s, s_s, w_s, acc_s = (refs[2 * i:2 * i + 2] for i in range(7))
    side = side_ref[0]
    copies = []
    for part in range(2):
        lane = pl.multiple_of(512 * part + 256 * side, 256)
        copies.append(pltpu.make_async_copy(
            all_ref.at[:, pl.ds(lane, 256)], kv_ref.at[:, pl.ds(256 * part, 256)], refs[14].at[part]
        ))
        copies[part].start()
    half_row = iota((RECV // 2, RECV), 0)
    half_col = iota((RECV // 2, RECV), 1)
    back_row = iota((RECV, RECV // 2), 0)
    back_col = iota((RECV, RECV // 2), 1)
    lanes = [(slice(kk * 128, (kk + 1) * 128), slice(256 + kk * 128, 256 + (kk + 1) * 128)) for kk in range(2)]

    def rows_of(i):
        return pl.ds(pl.multiple_of(i * BLOCK, BLOCK), BLOCK)

    def load(kk):
        take = one_hot(half_col == (half_row // 4) * 8 + kk * 4 + half_row % 4)
        for ref, first in ((q_s, 0), (c_s, 640)):
            ref[kk][0:RECV, :] = recv_ref[:, first + kk * 128:first + (kk + 1) * 128]
            ref[kk][RECV:2 * RECV, :] = recv_ref[:, first + 256 + kk * 128:first + 256 + (kk + 1) * 128]
            ref[kk][2 * RECV:QUERIES, :] = dot(take, recv_ref[:, first + 512:first + 640]).astype(bf16)
        qt_s[kk][...] = q_s[kk][...].astype(f32).T.astype(bf16)
        acc_s[kk][...] = jnp.zeros((HEAD_DIM, QUERIES), f32)

    def score(kk, i, top):
        s = dot(kv_ref[rows_of(i), lanes[kk][0]], qt_s[kk][...])
        s_s[kk][rows_of(i), :] = s
        return jnp.maximum(top, jnp.max(s, axis=0, keepdims=True))

    def weigh(kk, i, top, total):
        w = jnp.exp2(s_s[kk][rows_of(i), :] * EXP2_SCALE - top)
        wb = w.astype(bf16)
        w_s[kk][rows_of(i), :] = wb
        vt = kv_ref[rows_of(i), lanes[kk][1]].astype(f32).T.astype(bf16)
        acc_s[kk][...] += dot(vt, wb)
        return total + jnp.sum(w, axis=0, keepdims=True)

    def finish(kk, total):
        inverse = 1.0 / total
        out_t = acc_s[kk][...] * inverse
        ct = (c_s[kk][...].astype(f32).T * inverse).astype(bf16)
        ct_s[kk][...] = ct
        c_s[kk][...] = ct.astype(f32).T.astype(bf16)
        out = out_t.T.astype(bf16)
        out_ref[:, kk * 128:(kk + 1) * 128] = out[0:RECV, :]
        out_ref[:, 256 + kk * 128:256 + (kk + 1) * 128] = out[RECV:2 * RECV, :]
        give = one_hot(back_row == (back_col // 4) * 8 + kk * 4 + back_col % 4)
        return jnp.sum(ct.astype(f32) * out_t, axis=0, keepdims=True), dot(give, out[2 * RECV:QUERIES, :])

    def grads(kk, i, delta):
        key, val = lanes[kk]
        wb = w_s[kk][rows_of(i), :]
        prob_grad = dot(kv_ref[rows_of(i), val], ct_s[kk][...])
        ds = (wb.astype(f32) * (prob_grad - delta)).astype(bf16)
        value_grad = dot(wb, c_s[kk][...]).astype(bf16)
        key_grad = (dot(ds, q_s[kk][...]) * SCALE).astype(bf16)
        for sub in range(PAIR):
            first = i * BLOCK + lax.rem(side + sub, PAIR) * SHARD
            to = pl.ds(pl.multiple_of(first, SHARD), SHARD)
            here = slice(sub * SHARD, (sub + 1) * SHARD)
            grad_ref[to, val] = value_grad[here, :]
            grad_ref[to, key] = key_grad[here, :]

    steps = ROWS // BLOCK
    lowest = jnp.full((1, QUERIES), -jnp.inf, f32)
    zero = jnp.zeros((1, QUERIES), f32)

    load(0)
    load(1)
    for copy in copies:
        copy.wait()
    top0 = lax.fori_loop(0, steps, lambda i, top: score(0, i, top), lowest, unroll=UNROLL) * EXP2_SCALE

    def second(i, carry):
        top, total = carry
        return score(1, i, top), weigh(0, i, top0, total)

    top1, total0 = lax.fori_loop(0, steps, second, (lowest, zero), unroll=UNROLL)
    top1 = top1 * EXP2_SCALE
    delta0, tail0 = finish(0, total0)

    def third(i, total):
        grads(0, i, delta0)
        return weigh(1, i, top1, total)

    total1 = lax.fori_loop(0, steps, third, zero, unroll=UNROLL)
    delta1, tail1 = finish(1, total1)
    out_ref[:, 512:640] = (tail0 + tail1).astype(bf16)

    def fourth(i, carry):
        grads(1, i, delta1)
        return carry

    lax.fori_loop(0, steps, fourth, 0, unroll=UNROLL)


def join_kernel(side_ref, own_ref, other_ref, out_ref):
    def copy(ref, half):
        out_ref[:, half * 256:(half + 1) * 256] = ref[0:SHARD, 0:256].astype(f32)
        out_ref[:, 512 + half * 256:512 + (half + 1) * 256] = ref[0:SHARD, 256:512].astype(f32)

    for side in range(2):

        @pl.when(side_ref[0] == side)
        def _():
            copy(own_ref, side)
            copy(other_ref, 1 - side)


def vmem(count):
    return [pl.BlockSpec(memory_space=pltpu.VMEM)] * count


SMEM = pl.BlockSpec(memory_space=pltpu.SMEM)
WORK = [pltpu.VMEM((ROWS, 512), bf16)]
for shape, kind in (
    ((QUERIES, HEAD_DIM), bf16),
    ((QUERIES, HEAD_DIM), bf16),
    ((HEAD_DIM, QUERIES), bf16),
    ((HEAD_DIM, QUERIES), bf16),
    ((ROWS, QUERIES), f32),
    ((ROWS, QUERIES), bf16),
    ((HEAD_DIM, QUERIES), f32),
):
    WORK += [pltpu.VMEM(shape, kind)] * 2
WORK += [pltpu.SemaphoreType.DMA((2,))]
PARAMS = pltpu.CompilerParams(vmem_limit_bytes=VMEM_LIMIT)
ATTEND_COST = pl.CostEstimate(
    flops=2 * 5 * QUERIES * ROWS * HEAD_DIM * 2, bytes_accessed=6 * 1024 * 1024, transcendentals=2 * QUERIES * ROWS
)
SMALL_COST = pl.CostEstimate(flops=2 * 1024 * 1024 * 1024, bytes_accessed=3 * 1024 * 1024, transcendentals=0)


def local(queries, cotangent, corpus_of, cartridge):
    side = lax.axis_index("zl").astype(jnp.int32).reshape(1)
    swap = [(0, 1), (1, 0)]
    gathered = lax.all_gather(cartridge, ("zh", "zl"), axis=1, tiled=True)[0]

    col = corpus_of.astype(jnp.int32)
    row = col.reshape(1, TOK)
    packed = pl.pallas_call(
        pack_kernel,
        out_shape=jax.ShapeDtypeStruct((RECV, 1280), bf16),
        in_specs=vmem(4),
        out_specs=vmem(1)[0],
        compiler_params=PARAMS,
        cost_estimate=SMALL_COST,
        name="pack",
    )(row, col, queries, cotangent)
    recv = lax.all_to_all(packed, ("zl", "corpus"), split_axis=0, concat_axis=0, tiled=True)

    out, grads = pl.pallas_call(
        attend_kernel,
        out_shape=(jax.ShapeDtypeStruct((RECV, 640), bf16), jax.ShapeDtypeStruct((ROWS, 512), bf16)),
        in_specs=[SMEM] + vmem(1) + [pl.BlockSpec(memory_space=pl.ANY)],
        out_specs=tuple(vmem(2)),
        scratch_shapes=WORK,
        compiler_params=PARAMS,
        cost_estimate=ATTEND_COST,
        name="attend",
    )(side, recv, gathered)

    summed = lax.psum_scatter(grads, "zh", scatter_dimension=0, tiled=True)
    other = lax.ppermute(summed[SHARD:], "zl", swap)
    grad = pl.pallas_call(
        join_kernel,
        out_shape=jax.ShapeDtypeStruct((SHARD, 1024), f32),
        in_specs=[SMEM] + vmem(2),
        out_specs=vmem(1)[0],
        compiler_params=PARAMS,
        name="join",
    )(side, summed, other)

    replies = lax.all_to_all(out, ("zl", "corpus"), split_axis=0, concat_axis=0, tiled=True)
    attended = pl.pallas_call(
        unpack_kernel,
        out_shape=jax.ShapeDtypeStruct((TOK, 2048), bf16),
        in_specs=vmem(3),
        out_specs=vmem(1)[0],
        compiler_params=PARAMS,
        cost_estimate=SMALL_COST,
        name="unpack",
    )(row, col, replies)
    return attended, grad[None]


def solution(mesh):
    corpus, conv = mesh.devices.shape
    pairs = Mesh(mesh.devices.reshape(corpus, conv // PAIR, PAIR), ("corpus", "zh", "zl"))
    tokens = P(("corpus", "zh", "zl"), None)
    rows = P("corpus", ("zh", "zl"), None)
    return jax.shard_map(
        local,
        mesh=pairs,
        in_specs=(tokens, tokens, tokens, rows),
        out_specs=(tokens, rows),
        check_vma=False,
    )
```
